512 devices in a mesh: fsdp: 32 (over y, x, core), tp: 16 (over z).
Axes of the slice: x: 4, y: 4, z: 16, core: 2. Of those that a mesh axis runs over, the one named last changes fastest.
Arguments:
- gradient: float32 [18432, 7168], P('fsdp', 'tp'), may hold values from -600 to 600
- momentum: float32 [18432, 7168], P('fsdp', 'tp'), may hold values from -6 to 6
- start_basis: float32 [7168, 256], P('tp'), may hold values from -6 to 6
Outputs:
- update: float32 [18432, 7168], P('fsdp', 'tp')
- new_momentum: float32 [18432, 7168], P('fsdp', 'tp')
- directions: float32 [7168, 256], P('tp')
The draws below stay inside these ranges and needn't reach their ends.
All inputs are finite; a program needn't handle non-finite values.
Results may differ from the reference program's by a relative error of at most 0.00011.
Values sent between devices are 32-bit elements; how exact they have to be, the bound alone decides.
No kernel may reach another device: no remote copies, remote signals or barrier semaphores. Data moves between devices by JAX's collectives and lax.ppermute only.
A program may use at most 64 MiB of HBM per device.

```python
import math
import jax
import jax.numpy as jnp
from jax import lax

M_ROWS = 18432
N_COLS = 7168
RANK = 256
ITERS = 2


def draw_gradient(key, part):
    key = jax.random.fold_in(key, 11)
    keys = jax.random.split(key, 3)
    row_index = jnp.arange(M_ROWS, dtype=jnp.float32)[:, None]
    col_index = jnp.arange(N_COLS, dtype=jnp.float32)[None, :]
    row_scale = jnp.exp(jnp.log(3.0) * row_index / M_ROWS + jnp.log(3.33) * jax.random.uniform(keys[0], (M_ROWS, 1)))
    col_scale = jnp.exp(jnp.log(3.0) * col_index / N_COLS + jnp.log(3.33) * jax.random.uniform(keys[1], (1, N_COLS)))
    base = jnp.clip(jax.random.normal(keys[2], (M_ROWS, N_COLS)), -6.0, 6.0)
    return (base * row_scale * col_scale).astype(jnp.float32)


def block_levels(key, shape, cuts, smallest, top_value):
    def one(axis_at, parts):
        steps = jax.random.uniform(jax.random.fold_in(jax.random.fold_in(key, 6), axis_at), (parts,), jnp.float32, smallest / len(cuts), top_value / len(cuts))
        return jnp.repeat(jnp.exp(steps), shape[axis_at] // parts).reshape((-1,) + (1,) * (len(shape) - axis_at - 1))

    gain = one(*cuts[0])
    for cut in cuts[1:]:
        gain = gain * one(*cut)
    return gain


def scatter_about(key, shape, scale, reach, pieces=(), kind=jnp.bfloat16):
    entries = scale * jax.random.normal(key, shape, jnp.float32)
    if pieces:
        entries = entries * block_levels(key, shape, pieces, -0.22, 0.18)
    return jnp.clip(entries, -reach, reach).astype(kind)


def setup_inputs(seed: int = 0) -> dict:
    splits = jax.random.split(jax.random.key(seed), 4)
    gradient = draw_gradient(jax.random.fold_in(splits[3], 71), 0)
    momentum = scatter_about(splits[1], (M_ROWS, N_COLS), 1.0, 6.0, ((0, 32), (1, 16)), jnp.float32)
    start_basis = scatter_about(splits[2], (N_COLS, RANK), 1.0, 6.0, ((0, 16),), jnp.float32)
    return {"gradient": gradient, "momentum": momentum, "start_basis": start_basis}


decay_rate = 0.95
epsilon = 1e-06

def reference(gradient, momentum, start_basis):
    highest = lax.Precision.HIGHEST
    combined = momentum + gradient
    current = start_basis
    for iteration in range(ITERS):
        projected = jnp.dot(combined, current, precision=highest)
        gram_matrix = jnp.dot(projected.T, projected, precision=highest)
        factor = jnp.linalg.cholesky(gram_matrix)
        orthonormal = lax.linalg.triangular_solve(factor, projected, left_side=False, lower=True, transpose_a=True)
        reflected = jnp.dot(combined.T, orthonormal, precision=highest)
        current = reflected
    mean_square = lax.optimization_barrier(jnp.sum(reflected * reflected, axis=0)) / N_COLS
    directions = reflected * lax.rsqrt(mean_square + epsilon)
    new_momentum = combined - (1.0 - decay_rate) * jnp.dot(orthonormal, reflected.T, precision=highest)
    update = math.sqrt(M_ROWS / RANK) * jnp.dot(orthonormal, directions.T, precision=highest)
    return (update, new_momentum, directions)
```

```python
import math

import jax
import jax.numpy as jnp
from jax import lax
from jax.experimental import pallas as pl
from jax.experimental.pallas import tpu as pltpu
from jax.sharding import PartitionSpec as P

M_ROWS = 18432
N_COLS = 7168
RANK = 256
HALF = RANK // 2
FSDP = 32
TP = 16
ROWS = M_ROWS // FSDP
COLS = N_COLS // TP
BAND = 2 * ROWS // TP
SHARE = 40

decay_rate = 0.95
epsilon = 1e-06

F32 = jnp.float32
BF16 = jnp.bfloat16
HIGHEST = lax.Precision.HIGHEST
PANEL = 4

NN = (((1,), (0,)), ((), ()))
NT = (((1,), (1,)), ((), ()))
TN = (((0,), (0,)), ((), ()))


def split(x):
    high = x.astype(BF16)
    return high, (x - high.astype(F32)).astype(BF16)


def dot3(a, b, dims):
    one = lambda u, v: lax.dot_general(u, v, dims, preferred_element_type=F32)
    return one(a[0], b[0]) + (one(a[0], b[1]) + one(a[1], b[0]))


def dot6(a, b, dims):
    return lax.dot_general(a, b, dims, precision=HIGHEST, preferred_element_type=F32)


def call(kernel, out_shape, *args, flops=0, **kw):
    n_bytes = sum(x.size * x.dtype.itemsize for x in args)
    return pl.pallas_call(
        kernel,
        out_shape=out_shape,
        compiler_params=pltpu.CompilerParams(vmem_limit_bytes=48 * 2**20),
        cost_estimate=pl.CostEstimate(flops=flops, bytes_accessed=n_bytes, transcendentals=0),
        **kw,
    )(*args)


def shape(*dims, dtype=F32):
    return jax.ShapeDtypeStruct(dims, dtype)


def put_bands(ref, value):
    for i in range(value.shape[0] // BAND):
        for h in range(2):
            ref[2 * i + h] = value[i * BAND : (i + 1) * BAND, h * HALF : (h + 1) * HALF]


def get_bands(ref):
    halves = [ref[pl.ds(h, TP // 2, 2)] for h in range(2)]
    return jnp.concatenate([x.reshape(ROWS, HALF) for x in halves], axis=1)


def first_kernel(g_ref, m_ref, b_ref, high_ref, low_ref, out_ref):
    high, low = split(m_ref[...] + g_ref[...])
    high_ref[...] = high
    low_ref[...] = low
    put_bands(out_ref, dot3((high, low), split(b_ref[...]), NN))


def first(g, m, b):
    n = 4
    rows = ROWS // n
    block = pl.BlockSpec((rows, COLS), lambda i: (i, 0))
    return call(
        first_kernel,
        (shape(ROWS, COLS, dtype=BF16), shape(ROWS, COLS, dtype=BF16), shape(TP, BAND, HALF)),
        g,
        m,
        b,
        flops=6 * ROWS * COLS * RANK,
        grid=(n,),
        in_specs=[block, block, pl.BlockSpec((COLS, RANK), lambda i: (0, 0))],
        out_specs=[block, block, pl.BlockSpec((TP // n, BAND, HALF), lambda i: (i, 0, 0))],
    )


def fold_kernel(x_ref, out_ref):
    out_ref[...] = jnp.broadcast_to(jnp.sum(x_ref[...], axis=0, keepdims=True), out_ref.shape)


def all_sum(x, axis):
    terms = lax.all_to_all(x, axis, 0, 0)
    return lax.all_to_all(call(fold_kernel, shape(*x.shape), terms), axis, 0, 0)


def put_reflected(ref, c, p):
    for h in range(2):
        ref[h * COLS : (h + 1) * COLS, :] = c[:, h * HALF : (h + 1) * HALF]
    left, right = p[:, :HALF], p[:, HALF:]
    for i, (a, b) in enumerate(((left, left), (right, left), (right, right))):
        ref[2 * COLS + i * HALF : 2 * COLS + (i + 1) * HALF, :] = dot6(a, b, TN)


def get_reflected(ref):
    return jnp.concatenate([ref[h * COLS : (h + 1) * COLS, :] for h in range(2)], axis=1)


def reflect_kernel(high_ref, low_ref, p_ref, out_ref):
    p = get_bands(p_ref)
    put_reflected(out_ref, dot3((high_ref[...], low_ref[...]), split(p), TN), p)


def reflect(high, low, p):
    return call(reflect_kernel, shape(FSDP * SHARE, HALF), high, low, p, flops=6 * ROWS * COLS * RANK)


def project_kernel(high_ref, low_ref, c_ref, out_ref):
    put_bands(out_ref, dot3((high_ref[...], low_ref[...]), split(get_reflected(c_ref)), NN))


def project(high, low, c):
    return call(project_kernel, shape(TP, BAND, HALF), high, low, c, flops=6 * ROWS * COLS * RANK)


def second_reflect_kernel(high_ref, low_ref, p_ref, x_ref, p_out_ref, out_ref):
    p = dot6(get_bands(p_ref), x_ref[...], NT)
    p_out_ref[...] = p
    put_reflected(out_ref, dot3((high_ref[...], low_ref[...]), split(p), TN), p)


def second_reflect(high, low, p, x):
    return call(
        second_reflect_kernel,
        (shape(ROWS, RANK), shape(FSDP * SHARE, HALF)),
        high,
        low,
        p,
        x,
        flops=6 * ROWS * COLS * RANK,
    )


def inverse_factor_128(s):
    lanes = lambda v, k: jnp.broadcast_to(v[:, k : k + 1], (8, HALF))
    sublanes = lambda v, k: jnp.broadcast_to(v[k : k + 1, :], (8, HALF))
    n = HALF // 8
    a = [s[8 * v : 8 * v + 8, :] for v in range(n)]
    row_at = lax.broadcasted_iota(jnp.int32, (8, HALF), 0)
    col_at = lax.broadcasted_iota(jnp.int32, (8, HALF), 1)
    e = [jnp.where(col_at == row_at + 8 * v, 1.0, 0.0).astype(F32) for v in range(n)]
    out = []
    for k0 in range(0, HALF, PANEL):
        v0, s0 = k0 // 8, k0 % 8
        last = k0 + PANEL >= 8 * (v0 + 1)
        cols = {v: [lanes(a[v], k0 + j) for j in range(PANEL)] for v in range(v0, n)}
        rows = [sublanes(a[v0], s0 + j) for j in range(PANEL)]
        units = [sublanes(e[v0], s0 + j) for j in range(PANEL)]
        d = [[sublanes(cols[v0][j], s0 + i) for j in range(i + 1)] for i in range(PANEL)]
        factor = [[None] * PANEL for _ in range(PANEL)]
        inverse = [None] * PANEL
        for j in range(PANEL):
            t = d[j][j]
            for k in range(j):
                t = t - factor[j][k] * factor[j][k]
            r = lax.rsqrt(t)
            inverse[j] = r * (1.5 - 0.5 * t * (r * r))
            for i in range(j + 1, PANEL):
                t = d[i][j]
                for k in range(j):
                    t = t - factor[i][k] * factor[j][k]
                factor[i][j] = t * inverse[j]

        def solve(x):
            y = []
            for j in range(PANEL):
                t = x[j]
                for k in range(j):
                    t = t - factor[j][k] * y[k]
                y.append(t * inverse[j])
            return y

        rows, units = solve(rows), solve(units)
        out += [u[:1] for u in units]
        for v in range(v0 + 1 if last else v0, n):
            c = solve(cols[v])
            for j in range(PANEL):
                a[v] = a[v] - c[j] * rows[j]
                e[v] = e[v] - c[j] * units[j]
    return out


def store_rows(ref, at, rows):
    for i, row in enumerate(rows):
        ref[at + i : at + i + 1, :HALF] = row


def factor_kernel(g_ref, x_ref, t_ref):
    at = 2 * COLS
    g11, g21, g22 = (g_ref[at + i * HALF : at + (i + 1) * HALF, :] for i in range(3))
    store_rows(x_ref, 0, inverse_factor_128(g11))
    x_ref[:HALF, HALF:] = jnp.zeros((HALF, HALF), F32)
    x11 = x_ref[:HALF, :HALF]
    l21 = dot6(g21, x11, NT)
    store_rows(t_ref, 0, inverse_factor_128(g22 - dot6(l21, l21, NT)))
    x22 = t_ref[...]
    x_ref[HALF:, HALF:] = x22
    x_ref[HALF:, :HALF] = -dot6(x22, dot6(l21, x11, NN), NN)


def inverse_factor(reflected):
    return call(
        factor_kernel,
        shape(RANK, RANK),
        reflected,
        flops=2 * 10**10,
        scratch_shapes=[pltpu.VMEM((HALF, HALF), F32)],
    )


def basis_kernel(p_ref, c_ref, x_ref, q_ref, r_ref, s_ref):
    x = split(x_ref[...])
    q_ref[...] = dot3(split(p_ref[...]), x, NT)
    r = dot3(split(get_reflected(c_ref)), x, NT)
    r_ref[...] = r
    squares = jnp.sum(r * r, axis=0, keepdims=True)
    for h in range(2):
        half = squares[:, h * HALF : (h + 1) * HALF]
        s_ref[:, 4 * h : 4 * h + 4, :] = jnp.broadcast_to(half[None], (TP, 4, HALF))


def basis(p, c, x):
    return call(
        basis_kernel,
        (shape(ROWS, RANK), shape(COLS, RANK), shape(TP, 8, HALF)),
        p,
        c,
        x,
        flops=6 * (ROWS + COLS) * RANK * RANK,
    )


def momentum_kernel(g_ref, m_ref, q_ref, r_ref, out_ref):
    product = dot3(split(q_ref[...]), split(r_ref[...]), NT)
    out_ref[...] = (m_ref[...] + g_ref[...]) - (1.0 - decay_rate) * product


def update_kernel(q_ref, r_ref, s_ref, out_ref, d_ref):
    squares = jnp.sum(s_ref[...], axis=0)
    scale = lax.rsqrt(squares / N_COLS + epsilon)
    scale = jnp.concatenate([scale[:1], scale[4:5]], axis=1)
    d = r_ref[...] * scale
    d_ref[...] = d
    out_ref[...] = math.sqrt(M_ROWS / RANK) * dot3(split(q_ref[...]), split(d), NT)


def local(gradient, momentum, start_basis):
    high, low, p = first(gradient, momentum, start_basis)
    p = all_sum(p, "tp")
    c = reflect(high, low, p)
    c = all_sum(c.reshape(FSDP, SHARE, HALF), "fsdp").reshape(FSDP * SHARE, HALF)
    p = project(high, low, c)
    x = inverse_factor(c)
    p = all_sum(p, "tp")
    p, c = second_reflect(high, low, p, x)
    c = all_sum(c.reshape(FSDP, SHARE, HALF), "fsdp").reshape(FSDP * SHARE, HALF)
    x = inverse_factor(c)
    q, r, squares = basis(p, c, x)
    squares = lax.all_to_all(squares, "tp", 0, 0)
    flops = 6 * ROWS * COLS * RANK
    new_momentum = call(momentum_kernel, shape(ROWS, COLS), gradient, momentum, q, r, flops=flops)
    update, directions = call(
        update_kernel, (shape(ROWS, COLS), shape(COLS, RANK)), q, r, squares, flops=flops
    )
    return (update, new_momentum, directions)


def solution(mesh):
    return jax.shard_map(
        local,
        mesh=mesh,
        in_specs=(P("fsdp", "tp"), P("fsdp", "tp"), P("tp", None)),
        out_specs=(P("fsdp", "tp"), P("fsdp", "tp"), P("tp", None)),
        check_vma=False,
    )
```

```python
import math

import jax
import jax.numpy as jnp
from jax import lax
from jax.experimental import pallas as pl
from jax.experimental.pallas import tpu as pltpu
from jax.sharding import PartitionSpec as P

M_ROWS = 18432
N_COLS = 7168
RANK = 256
HALF = RANK // 2
FSDP = 32
TP = 16
ROWS = M_ROWS // FSDP
COLS = N_COLS // TP
BAND = 2 * ROWS // TP
SHARE = 40

decay_rate = 0.95
epsilon = 1e-06

F32 = jnp.float32
BF16 = jnp.bfloat16
HIGHEST = lax.Precision.HIGHEST
PANEL = 8

NN = (((1,), (0,)), ((), ()))
NT = (((1,), (1,)), ((), ()))
TN = (((0,), (0,)), ((), ()))


def split(x):
    high = x.astype(BF16)
    return high, (x - high.astype(F32)).astype(BF16)


def dot3(a, b, dims):
    one = lambda u, v: lax.dot_general(u, v, dims, preferred_element_type=F32)
    return one(a[0], b[0]) + (one(a[0], b[1]) + one(a[1], b[0]))


def dot6(a, b, dims):
    return lax.dot_general(a, b, dims, precision=HIGHEST, preferred_element_type=F32)


def call(kernel, out_shape, *args, flops=0, vmem=48, **kw):
    n_bytes = sum(x.size * x.dtype.itemsize for x in args)
    return pl.pallas_call(
        kernel,
        out_shape=out_shape,
        compiler_params=pltpu.CompilerParams(vmem_limit_bytes=vmem * 2**20),
        cost_estimate=pl.CostEstimate(flops=flops, bytes_accessed=n_bytes, transcendentals=0),
        **kw,
    )(*args)


def shape(*dims, dtype=F32):
    return jax.ShapeDtypeStruct(dims, dtype)


def put_halves(own_ref, other_ref, value):
    left, right = value[:, :HALF], value[:, HALF:]
    even = lax.rem(lax.axis_index("tp"), 2) == 0
    own_ref[...] = jnp.where(even, left, right)
    other_ref[...] = jnp.where(even, right, left)


def get_bands(ref):
    halves = [ref[pl.ds(h, TP // 2, 2)] for h in range(2)]
    return jnp.concatenate([x.reshape(ROWS, HALF) for x in halves], axis=1)


def first_kernel(g_ref, m_ref, b_ref, high_ref, low_ref, own_ref, other_ref, total_ref):
    step = pl.program_id(0)
    high, low = split(m_ref[...] + g_ref[...])
    high_ref[...] = high
    low_ref[...] = low
    term = dot3((high, low), split(b_ref[...]), TN)

    @pl.when(step == 0)
    def _():
        total_ref[...] = term

    @pl.when(step > 0)
    def _():
        total_ref[...] += term

    @pl.when(step == pl.num_programs(0) - 1)
    def _():
        put_halves(own_ref, other_ref, total_ref[...])


def first(g, m, b):
    n = 4
    wide = shape(COLS, ROWS, dtype=BF16)
    half = shape(ROWS, HALF)
    block = pl.BlockSpec((COLS // n, ROWS), lambda i: (i, 0))
    whole = pl.BlockSpec((ROWS, HALF), lambda i: (0, 0))
    return call(
        first_kernel,
        (wide, wide, half, half),
        g,
        m,
        b,
        flops=6 * ROWS * COLS * RANK,
        vmem=60,
        grid=(n,),
        in_specs=[block, block, pl.BlockSpec((COLS // n, RANK), lambda i: (i, 0))],
        out_specs=[block, block, whole, whole],
        scratch_shapes=[pltpu.VMEM((ROWS, RANK), F32)],
    )


def fold_kernel(x_ref, out_ref):
    out_ref[...] = jnp.broadcast_to(jnp.sum(x_ref[...], axis=0, keepdims=True), out_ref.shape)


def all_sum(x, axis):
    terms = lax.all_to_all(x, axis, 0, 0)
    return lax.all_to_all(call(fold_kernel, shape(*x.shape), terms), axis, 0, 0)


def band_kernel(x_ref, out_ref):
    out_ref[...] = jnp.sum(x_ref[...], axis=0)


def tp_sum(own, other, beside=None):
    own = own + lax.ppermute(other, "tp", [(i, i ^ 1) for i in range(TP)])
    places = [list(range(i, TP, 2)) for i in range(2)]
    terms = lax.all_to_all(own.reshape(TP // 2, BAND, HALF), "tp", 0, 0, axis_index_groups=places)
    band = call(band_kernel, shape(BAND, HALF), terms)
    if beside is not None:
        band, beside = lax.optimization_barrier((band, beside))
    return lax.all_gather(band, "tp"), beside


def put_reflected(ref, c, p):
    for h in range(2):
        ref[h * COLS : (h + 1) * COLS, :] = c[:, h * HALF : (h + 1) * HALF]
    left, right = p[:, :HALF], p[:, HALF:]
    for i, (a, b) in enumerate(((left, left), (right, left), (right, right))):
        ref[2 * COLS + i * HALF : 2 * COLS + (i + 1) * HALF, :] = dot6(a, b, TN)


def get_reflected(ref):
    return jnp.concatenate([ref[h * COLS : (h + 1) * COLS, :] for h in range(2)], axis=1)


def reflect_kernel(high_ref, low_ref, p_ref, out_ref):
    p = get_bands(p_ref)
    put_reflected(out_ref, dot3((high_ref[...], low_ref[...]), split(p), NN), p)


def reflect(high, low, p):
    return call(reflect_kernel, shape(FSDP * SHARE, HALF), high, low, p, flops=6 * ROWS * COLS * RANK)


def project_kernel(high_ref, low_ref, c_ref, own_ref, other_ref):
    c = split(get_reflected(c_ref))
    put_halves(own_ref, other_ref, dot3((high_ref[...], low_ref[...]), c, TN))


def project(high, low, c):
    half = shape(ROWS, HALF)
    return call(project_kernel, (half, half), high, low, c, flops=6 * ROWS * COLS * RANK)


def second_reflect_kernel(high_ref, low_ref, p_ref, x_ref, p_out_ref, out_ref):
    p = dot3(split(get_bands(p_ref)), split(x_ref[...]), NT)
    p_out_ref[...] = p
    put_reflected(out_ref, dot3((high_ref[...], low_ref[...]), split(p), NN), p)


def second_reflect(high, low, p, x):
    return call(
        second_reflect_kernel,
        (shape(ROWS, RANK), shape(FSDP * SHARE, HALF)),
        high,
        low,
        p,
        x,
        flops=6 * ROWS * COLS * RANK,
    )


def inverse_factor_128(s):
    lanes = lambda v, k: jnp.broadcast_to(v[:, k : k + 1], (8, HALF))
    sublanes = lambda v, k: jnp.broadcast_to(v[k : k + 1, :], (8, HALF))
    n = HALF // 8
    a = [s[8 * v : 8 * v + 8, :] for v in range(n)]
    row_at = lax.broadcasted_iota(jnp.int32, (8, HALF), 0)
    col_at = lax.broadcasted_iota(jnp.int32, (8, HALF), 1)
    e = [jnp.where(col_at == row_at + 8 * v, 1.0, 0.0).astype(F32) for v in range(n)]
    out = []
    for k0 in range(0, HALF, PANEL):
        place = [divmod(k0 + j, 8) for j in range(PANEL)]
        cols = {v: [lanes(a[v], k0 + j) for j in range(PANEL)] for v in range(k0 // 8, n)}
        rows = [sublanes(a[v], k) for v, k in place]
        units = [sublanes(e[v], k) for v, k in place]
        d = [[sublanes(cols[v][j], k) for j in range(i + 1)] for i, (v, k) in enumerate(place)]
        factor = [[None] * PANEL for _ in range(PANEL)]
        inverse = [None] * PANEL
        for j in range(PANEL):
            t = d[j][j]
            for k in range(j):
                t = t - factor[j][k] * factor[j][k]
            inverse[j] = lax.rsqrt(t)
            for i in range(j + 1, PANEL):
                t = d[i][j]
                for k in range(j):
                    t = t - factor[i][k] * factor[j][k]
                factor[i][j] = t * inverse[j]

        def solve(x):
            y = []
            for j in range(PANEL):
                t = x[j]
                for k in range(j):
                    t = t - factor[j][k] * y[k]
                y.append(t * inverse[j])
            return y

        rows, units = solve(rows), solve(units)
        out += [u[:1] for u in units]
        for v in range((k0 + PANEL) // 8, n):
            c = solve(cols[v])
            for j in range(PANEL):
                a[v] = a[v] - c[j] * rows[j]
                e[v] = e[v] - c[j] * units[j]
    return out


def store_rows(ref, at, rows):
    for i, row in enumerate(rows):
        ref[at + i : at + i + 1, :HALF] = row


def factor_kernel(g_ref, x_ref, t_ref):
    at = 2 * COLS
    g11, g21, g22 = (g_ref[at + i * HALF : at + (i + 1) * HALF, :] for i in range(3))
    store_rows(x_ref, 0, inverse_factor_128(g11))
    x_ref[:HALF, HALF:] = jnp.zeros((HALF, HALF), F32)
    x11 = x_ref[:HALF, :HALF]
    l21 = dot6(g21, x11, NT)
    store_rows(t_ref, 0, inverse_factor_128(g22 - dot6(l21, l21, NT)))
    x22 = t_ref[...]
    x_ref[HALF:, HALF:] = x22
    x_ref[HALF:, :HALF] = -dot6(x22, dot6(l21, x11, NN), NN)


def inverse_factor(reflected):
    return call(
        factor_kernel,
        shape(RANK, RANK),
        reflected,
        flops=2 * 10**10,
        scratch_shapes=[pltpu.VMEM((HALF, HALF), F32)],
    )


def basis_kernel(p_ref, c_ref, x_ref, q_ref, r_ref, s_ref):
    x = split(x_ref[...])
    q_ref[...] = dot3(split(p_ref[...]), x, NT)
    r = dot3(split(get_reflected(c_ref)), x, NT)
    r_ref[...] = r
    squares = jnp.sum(r * r, axis=0, keepdims=True)
    for h in range(2):
        half = squares[:, h * HALF : (h + 1) * HALF]
        s_ref[:, 4 * h : 4 * h + 4, :] = jnp.broadcast_to(half[None], (TP, 4, HALF))


def basis(p, c, x):
    return call(
        basis_kernel,
        (shape(ROWS, RANK), shape(COLS, RANK), shape(TP, 8, HALF)),
        p,
        c,
        x,
        flops=6 * (ROWS + COLS) * RANK * RANK,
    )


def momentum_kernel(g_ref, m_ref, q_ref, r_ref, out_ref):
    product = dot3(split(r_ref[...]), split(q_ref[...]), NT)
    out_ref[...] = (m_ref[...] + g_ref[...]) - (1.0 - decay_rate) * product


def update_kernel(q_ref, r_ref, s_ref, out_ref, d_ref):
    squares = jnp.sum(s_ref[...], axis=0)
    scale = lax.rsqrt(squares / N_COLS + epsilon)
    scale = jnp.concatenate([scale[:1], scale[4:5]], axis=1)
    d = r_ref[...] * scale
    d_ref[...] = d
    out_ref[...] = math.sqrt(M_ROWS / RANK) * dot3(split(d), split(q_ref[...]), NT)


def local(gradient, momentum, start_basis):
    gradient, momentum = gradient.T, momentum.T
    high, low, *p = first(gradient, momentum, start_basis)
    p, _ = tp_sum(*p)
    c = reflect(high, low, p)
    c = all_sum(c.reshape(FSDP, SHARE, HALF), "fsdp").reshape(FSDP * SHARE, HALF)
    p = project(high, low, c)
    p, x = tp_sum(*p, inverse_factor(c))
    p, c = second_reflect(high, low, p, x)
    c = all_sum(c.reshape(FSDP, SHARE, HALF), "fsdp").reshape(FSDP * SHARE, HALF)
    x = inverse_factor(c)
    q, r, squares = basis(p, c, x)
    squares = lax.all_to_all(squares, "tp", 0, 0)
    flops = 6 * ROWS * COLS * RANK
    new_momentum = call(momentum_kernel, shape(COLS, ROWS), gradient, momentum, q, r, flops=flops)
    update, directions = call(
        update_kernel, (shape(COLS, ROWS), shape(COLS, RANK)), q, r, squares, flops=flops
    )
    return (update.T, new_momentum.T, directions)


def solution(mesh):
    return jax.shard_map(
        local,
        mesh=mesh,
        in_specs=(P("fsdp", "tp"), P("fsdp", "tp"), P("tp", None)),
        out_specs=(P("fsdp", "tp"), P("fsdp", "tp"), P("tp", None)),
        check_vma=False,
    )
```

```python
import math

import jax
import jax.numpy as jnp
from jax import lax
from jax.experimental import pallas as pl
from jax.experimental.pallas import tpu as pltpu
from jax.sharding import PartitionSpec as P

M_ROWS = 18432
N_COLS = 7168
RANK = 256
HALF = RANK // 2
FSDP = 32
TP = 16
ROWS = M_ROWS // FSDP
COLS = N_COLS // TP
BAND = 2 * ROWS // TP
SHARE = 40

decay_rate = 0.95
epsilon = 1e-06

F32 = jnp.float32
BF16 = jnp.bfloat16
HIGHEST = lax.Precision.HIGHEST
PANEL = 8
RUN = 4

NN = (((1,), (0,)), ((), ()))
NT = (((1,), (1,)), ((), ()))
TN = (((0,), (0,)), ((), ()))


def split(x):
    high = x.astype(BF16)
    return high, (x - high.astype(F32)).astype(BF16)


def dot3(a, b, dims):
    one = lambda u, v: lax.dot_general(u, v, dims, preferred_element_type=F32)
    return one(a[0], b[0]) + (one(a[0], b[1]) + one(a[1], b[0]))


def dot6(a, b, dims):
    return lax.dot_general(a, b, dims, precision=HIGHEST, preferred_element_type=F32)


def call(kernel, out_shape, *args, flops=0, vmem=48, **kw):
    n_bytes = sum(x.size * x.dtype.itemsize for x in args)
    return pl.pallas_call(
        kernel,
        out_shape=out_shape,
        compiler_params=pltpu.CompilerParams(vmem_limit_bytes=vmem * 2**20),
        cost_estimate=pl.CostEstimate(flops=flops, bytes_accessed=n_bytes, transcendentals=0),
        **kw,
    )(*args)


def shape(*dims, dtype=F32):
    return jax.ShapeDtypeStruct(dims, dtype)


def put_bands(ref, value):
    for i in range(ROWS // BAND):
        for h in range(2):
            run, place = divmod(2 * i + h, RUN)
            ref[place * RUN + run] = value[i * BAND : (i + 1) * BAND, h * HALF : (h + 1) * HALF]


def get_bands(ref):
    halves = [ref[pl.ds(h, TP // 2, 2)] for h in range(2)]
    return jnp.concatenate([x.reshape(ROWS, HALF) for x in halves], axis=1)


def first_kernel(g_ref, m_ref, b_ref, high_ref, low_ref, out_ref):
    high, low = split(m_ref[...] + g_ref[...])
    high_ref[...] = high
    low_ref[...] = low
    put_bands(out_ref, dot3((high, low), split(b_ref[...]), TN))


def first(g, m, b):
    wide = shape(COLS, ROWS, dtype=BF16)
    return call(
        first_kernel, (wide, wide, shape(TP, BAND, HALF)), g, m, b, flops=6 * ROWS * COLS * RANK
    )


def fold_kernel(x_ref, out_ref):
    out_ref[...] = jnp.broadcast_to(jnp.sum(x_ref[...], axis=0, keepdims=True), out_ref.shape)


def all_sum(x, axis):
    terms = lax.all_to_all(x, axis, 0, 0)
    return lax.all_to_all(call(fold_kernel, shape(*x.shape), terms), axis, 0, 0)


def add_kernel(x_ref, out_ref):
    out_ref[...] = jnp.sum(x_ref[...], axis=0)


def tp_sum(x, beside=None):
    near = [list(range(i, i + RUN)) for i in range(0, TP, RUN)]
    far = [list(range(i, TP, RUN)) for i in range(RUN)]
    x = lax.all_to_all(x.reshape(RUN, RUN * BAND, HALF), "tp", 0, 0, axis_index_groups=near)
    x = call(add_kernel, shape(RUN * BAND, HALF), x).reshape(RUN, BAND, HALF)
    x = lax.all_to_all(x, "tp", 0, 0, axis_index_groups=far)
    band = call(add_kernel, shape(BAND, HALF), x)
    if beside is not None:
        band, beside = lax.optimization_barrier((band, beside))
    return lax.all_gather(band, "tp"), beside


def put_reflected(ref, c, p):
    for h in range(2):
        ref[h * COLS : (h + 1) * COLS, :] = c[:, h * HALF : (h + 1) * HALF]
    left, right = p[:, :HALF], p[:, HALF:]
    for i, (a, b) in enumerate(((left, left), (right, left), (right, right))):
        ref[2 * COLS + i * HALF : 2 * COLS + (i + 1) * HALF, :] = dot6(a, b, TN)


def get_reflected(ref):
    return jnp.concatenate([ref[h * COLS : (h + 1) * COLS, :] for h in range(2)], axis=1)


def reflect_kernel(high_ref, low_ref, p_ref, out_ref):
    p = get_bands(p_ref)
    put_reflected(out_ref, dot3((high_ref[...], low_ref[...]), split(p), NN), p)


def reflect(high, low, p):
    return call(reflect_kernel, shape(FSDP * SHARE, HALF), high, low, p, flops=6 * ROWS * COLS * RANK)


def project_kernel(high_ref, low_ref, c_ref, out_ref):
    put_bands(out_ref, dot3((high_ref[...], low_ref[...]), split(get_reflected(c_ref)), TN))


def project(high, low, c):
    return call(project_kernel, shape(TP, BAND, HALF), high, low, c, flops=6 * ROWS * COLS * RANK)


def second_reflect_kernel(high_ref, low_ref, p_ref, x_ref, p_out_ref, out_ref):
    p = dot3(split(get_bands(p_ref)), split(x_ref[...]), NT)
    p_out_ref[...] = p
    put_reflected(out_ref, dot3((high_ref[...], low_ref[...]), split(p), NN), p)


def second_reflect(high, low, p, x):
    return call(
        second_reflect_kernel,
        (shape(ROWS, RANK), shape(FSDP * SHARE, HALF)),
        high,
        low,
        p,
        x,
        flops=6 * ROWS * COLS * RANK,
    )


def inverse_factor_128(s):
    lanes = lambda v, k: jnp.broadcast_to(v[:, k : k + 1], (8, HALF))
    sublanes = lambda v, k: jnp.broadcast_to(v[k : k + 1, :], (8, HALF))
    n = HALF // 8
    a = [s[8 * v : 8 * v + 8, :] for v in range(n)]
    row_at = lax.broadcasted_iota(jnp.int32, (8, HALF), 0)
    col_at = lax.broadcasted_iota(jnp.int32, (8, HALF), 1)
    e = [jnp.where(col_at == row_at + 8 * v, 1.0, 0.0).astype(F32) for v in range(n)]
    out = []
    for k0 in range(0, HALF, PANEL):
        place = [divmod(k0 + j, 8) for j in range(PANEL)]
        cols = {v: [lanes(a[v], k0 + j) for j in range(PANEL)] for v in range(k0 // 8, n)}
        rows = [sublanes(a[v], k) for v, k in place]
        units = [sublanes(e[v], k) for v, k in place]
        d = [[sublanes(cols[v][j], k) for j in range(i + 1)] for i, (v, k) in enumerate(place)]
        factor = [[None] * PANEL for _ in range(PANEL)]
        inverse = [None] * PANEL
        for j in range(PANEL):
            t = d[j][j]
            for k in range(j):
                t = t - factor[j][k] * factor[j][k]
            inverse[j] = lax.rsqrt(t)
            for i in range(j + 1, PANEL):
                t = d[i][j]
                for k in range(j):
                    t = t - factor[i][k] * factor[j][k]
                factor[i][j] = t * inverse[j]

        def solve(x):
            y = []
            for j in range(PANEL):
                t = x[j]
                for k in range(j):
                    t = t - factor[j][k] * y[k]
                y.append(t * inverse[j])
            return y

        rows, units = solve(rows), solve(units)
        out += [u[:1] for u in units]
        for v in range((k0 + PANEL) // 8, n):
            c = solve(cols[v])
            for j in range(PANEL):
                a[v] = a[v] - c[j] * rows[j]
                e[v] = e[v] - c[j] * units[j]
    return out


def store_rows(ref, at, rows):
    for i, row in enumerate(rows):
        ref[at + i : at + i + 1, :HALF] = row


def factor_kernel(g_ref, x_ref, t_ref):
    at = 2 * COLS
    g11, g21, g22 = (g_ref[at + i * HALF : at + (i + 1) * HALF, :] for i in range(3))
    store_rows(x_ref, 0, inverse_factor_128(g11))
    x_ref[:HALF, HALF:] = jnp.zeros((HALF, HALF), F32)
    x11 = x_ref[:HALF, :HALF]
    l21 = dot6(g21, x11, NT)
    store_rows(t_ref, 0, inverse_factor_128(g22 - dot6(l21, l21, NT)))
    x22 = t_ref[...]
    x_ref[HALF:, HALF:] = x22
    x_ref[HALF:, :HALF] = -dot6(x22, dot6(l21, x11, NN), NN)


def inverse_factor(reflected):
    return call(
        factor_kernel,
        shape(RANK, RANK),
        reflected,
        flops=2 * 10**10,
        scratch_shapes=[pltpu.VMEM((HALF, HALF), F32)],
    )


def right_kernel(c_ref, x_ref, r_ref, s_ref):
    r = dot3(split(get_reflected(c_ref)), split(x_ref[...]), NT)
    r_ref[...] = r
    squares = jnp.sum(r * r, axis=0, keepdims=True)
    for h in range(2):
        half = squares[:, h * HALF : (h + 1) * HALF]
        s_ref[:, 4 * h : 4 * h + 4, :] = jnp.broadcast_to(half[None], (TP, 4, HALF))


def right(c, x):
    return call(
        right_kernel, (shape(COLS, RANK), shape(TP, 8, HALF)), c, x, flops=6 * COLS * RANK * RANK
    )


def left_kernel(p_ref, x_ref, q_ref):
    q_ref[...] = dot3(split(p_ref[...]), split(x_ref[...]), NT)


def momentum_kernel(g_ref, m_ref, q_ref, r_ref, out_ref):
    product = dot3(split(r_ref[...]), split(q_ref[...]), NT)
    out_ref[...] = (m_ref[...] + g_ref[...]) - (1.0 - decay_rate) * product


def update_kernel(q_ref, r_ref, s_ref, out_ref, d_ref):
    squares = jnp.sum(s_ref[...], axis=0)
    scale = lax.rsqrt(squares / N_COLS + epsilon)
    scale = jnp.concatenate([scale[:1], scale[4:5]], axis=1)
    d = r_ref[...] * scale
    d_ref[...] = d
    out_ref[...] = math.sqrt(M_ROWS / RANK) * dot3(split(d), split(q_ref[...]), NT)


def local(gradient, momentum, start_basis):
    gradient, momentum = gradient.T, momentum.T
    high, low, p = first(gradient, momentum, start_basis)
    p, _ = tp_sum(p)
    c = reflect(high, low, p)
    c = all_sum(c.reshape(FSDP, SHARE, HALF), "fsdp").reshape(FSDP * SHARE, HALF)
    p = project(high, low, c)
    p, x = tp_sum(p, inverse_factor(c))
    p, c = second_reflect(high, low, p, x)
    c = all_sum(c.reshape(FSDP, SHARE, HALF), "fsdp").reshape(FSDP * SHARE, HALF)
    x = inverse_factor(c)
    r, squares = right(c, x)
    squares = lax.all_to_all(squares, "tp", 0, 0)
    q = call(left_kernel, shape(ROWS, RANK), p, x, flops=6 * ROWS * RANK * RANK)
    flops = 6 * ROWS * COLS * RANK
    new_momentum = call(momentum_kernel, shape(COLS, ROWS), gradient, momentum, q, r, flops=flops)
    update, directions = call(
        update_kernel, (shape(COLS, ROWS), shape(COLS, RANK)), q, r, squares, flops=flops
    )
    return (update.T, new_momentum.T, directions)


def solution(mesh):
    return jax.shard_map(
        local,
        mesh=mesh,
        in_specs=(P("fsdp", "tp"), P("fsdp", "tp"), P("tp", None)),
        out_specs=(P("fsdp", "tp"), P("fsdp", "tp"), P("tp", None)),
        check_vma=False,
    )
```

```python
import math

import jax
import jax.numpy as jnp
from jax import lax
from jax.experimental import pallas as pl
from jax.experimental.pallas import tpu as pltpu
from jax.sharding import PartitionSpec as P

M_ROWS = 18432
N_COLS = 7168
RANK = 256
HALF = RANK // 2
FSDP = 32
TP = 16
ROWS = M_ROWS // FSDP
COLS = N_COLS // TP
BAND = 2 * ROWS // TP
PACKED = 2 * COLS + 3 * HALF

decay_rate = 0.95
epsilon = 1e-06

F32 = jnp.float32
BF16 = jnp.bfloat16
HIGHEST = lax.Precision.HIGHEST
PANEL = 8

NN = (((1,), (0,)), ((), ()))
NT = (((1,), (1,)), ((), ()))
TN = (((0,), (0,)), ((), ()))


def split(x):
    high = x.astype(BF16)
    return high, (x - high.astype(F32)).astype(BF16)


def dot3(a, b, dims):
    one = lambda u, v: lax.dot_general(u, v, dims, preferred_element_type=F32)
    return one(a[0], b[0]) + (one(a[0], b[1]) + one(a[1], b[0]))


def dot6(a, b, dims):
    return lax.dot_general(a, b, dims, precision=HIGHEST, preferred_element_type=F32)


def call(kernel, out_shape, *args, flops=0, vmem=48, **kw):
    n_bytes = sum(x.size * x.dtype.itemsize for x in args)
    return pl.pallas_call(
        kernel,
        out_shape=out_shape,
        compiler_params=pltpu.CompilerParams(vmem_limit_bytes=vmem * 2**20),
        cost_estimate=pl.CostEstimate(flops=flops, bytes_accessed=n_bytes, transcendentals=0),
        **kw,
    )(*args)


def shape(*dims, dtype=F32):
    return jax.ShapeDtypeStruct(dims, dtype)


def put_halves(own_ref, other_ref, value):
    left, right = value[:, :HALF], value[:, HALF:]
    even = lax.rem(lax.axis_index("tp"), 2) == 0
    own_ref[...] = jnp.where(even, left, right)
    other_ref[...] = jnp.where(even, right, left)


def get_bands(ref):
    halves = [ref[pl.ds(h, TP // 2, 2)] for h in range(2)]
    return jnp.concatenate([x.reshape(ROWS, HALF) for x in halves], axis=1)


def first_kernel(g_ref, m_ref, b_ref, high_ref, low_ref, own_ref, other_ref):
    high, low = split(m_ref[...] + g_ref[...])
    high_ref[...] = high
    low_ref[...] = low
    put_halves(own_ref, other_ref, dot3((high, low), split(b_ref[...]), TN))


def first(g, m, b):
    wide = shape(COLS, ROWS, dtype=BF16)
    half = shape(ROWS, HALF)
    return call(first_kernel, (wide, wide, half, half), g, m, b, flops=6 * ROWS * COLS * RANK)


def add_kernel(x_ref, out_ref):
    out_ref[...] = jnp.sum(x_ref[...], axis=0)


def repeat_kernel(x_ref, y_ref, out_ref):
    out_ref[...] = jnp.broadcast_to((x_ref[...] + y_ref[...])[None], out_ref.shape)


def fsdp_sum(x):
    chips = FSDP // 2
    places = [list(range(core, FSDP, 2)) for core in range(2)]
    rows = x.shape[0] // chips
    terms = lax.all_to_all(x.reshape(chips, rows, HALF), "fsdp", 0, 0, axis_index_groups=places)
    piece = call(add_kernel, shape(rows, HALF), terms)
    other = lax.ppermute(piece, "fsdp", [(i, i ^ 1) for i in range(FSDP)])
    pieces = call(repeat_kernel, shape(chips, rows, HALF), piece, other)
    pieces = lax.all_to_all(pieces, "fsdp", 0, 0, axis_index_groups=places)
    return pieces.reshape(chips * rows, HALF)


def tp_sum(own, other, beside=None):
    own = own + lax.ppermute(other, "tp", [(i, i ^ 1) for i in range(TP)])
    places = [list(range(i, TP, 2)) for i in range(2)]
    terms = lax.all_to_all(own.reshape(TP // 2, BAND, HALF), "tp", 0, 0, axis_index_groups=places)
    band = call(add_kernel, shape(BAND, HALF), terms)
    if beside is not None:
        band, beside = lax.optimization_barrier((band, beside))
    return lax.all_gather(band, "tp"), beside


def put_reflected(ref, c, p):
    for h in range(2):
        ref[h * COLS : (h + 1) * COLS, :] = c[:, h * HALF : (h + 1) * HALF]
    left, right = p[:, :HALF], p[:, HALF:]
    for i, (a, b) in enumerate(((left, left), (right, left), (right, right))):
        ref[2 * COLS + i * HALF : 2 * COLS + (i + 1) * HALF, :] = dot6(a, b, TN)


def get_reflected(ref):
    return jnp.concatenate([ref[h * COLS : (h + 1) * COLS, :] for h in range(2)], axis=1)


def reflect_kernel(high_ref, low_ref, p_ref, out_ref):
    p = get_bands(p_ref)
    put_reflected(out_ref, dot3((high_ref[...], low_ref[...]), split(p), NN), p)


def reflect(high, low, p):
    return call(reflect_kernel, shape(PACKED, HALF), high, low, p, flops=6 * ROWS * COLS * RANK)


def project_kernel(high_ref, low_ref, c_ref, own_ref, other_ref):
    c = split(get_reflected(c_ref))
    put_halves(own_ref, other_ref, dot3((high_ref[...], low_ref[...]), c, TN))


def project(high, low, c):
    half = shape(ROWS, HALF)
    return call(project_kernel, (half, half), high, low, c, flops=6 * ROWS * COLS * RANK)


def second_reflect_kernel(high_ref, low_ref, p_ref, x_ref, p_out_ref, out_ref):
    p = dot3(split(get_bands(p_ref)), split(x_ref[...]), NT)
    p_out_ref[...] = p
    put_reflected(out_ref, dot3((high_ref[...], low_ref[...]), split(p), NN), p)


def second_reflect(high, low, p, x):
    return call(
        second_reflect_kernel,
        (shape(ROWS, RANK), shape(PACKED, HALF)),
        high,
        low,
        p,
        x,
        flops=6 * ROWS * COLS * RANK,
    )


def inverse_factor_128(s):
    lanes = lambda v, k: jnp.broadcast_to(v[:, k : k + 1], (8, HALF))
    sublanes = lambda v, k: jnp.broadcast_to(v[k : k + 1, :], (8, HALF))
    n = HALF // 8
    col_at = lax.broadcasted_iota(jnp.int32, (8, HALF), 1)
    a = [s[8 * v : 8 * v + 8, :] for v in range(n)]
    out = []
    for k0 in range(0, HALF, PANEL):
        place = [divmod(k0 + j, 8) for j in range(PANEL)]
        in_panel = (col_at >= k0) & (col_at < k0 + PANEL)
        cols = {v: [lanes(a[v], k0 + j) for j in range(PANEL)] for v in range(k0 // 8, n)}
        rows = [
            jnp.where(in_panel, jnp.where(col_at == k0 + j, 1.0, 0.0), sublanes(a[v], k))
            for j, (v, k) in enumerate(place)
        ]
        d = [[sublanes(cols[v][j], k) for j in range(i + 1)] for i, (v, k) in enumerate(place)]
        factor = [[None] * PANEL for _ in range(PANEL)]
        inverse = [None] * PANEL
        for j in range(PANEL):
            t = d[j][j]
            for k in range(j):
                t = t - factor[j][k] * factor[j][k]
            inverse[j] = lax.rsqrt(t)
            for i in range(j + 1, PANEL):
                t = d[i][j]
                for k in range(j):
                    t = t - factor[i][k] * factor[j][k]
                factor[i][j] = t * inverse[j]

        def solve(x):
            y = []
            for j in range(PANEL):
                t = x[j]
                for k in range(j):
                    t = t - factor[j][k] * y[k]
                y.append(t * inverse[j])
            return y

        rows = solve(rows)
        out += [jnp.where(col_at < k0 + PANEL, row, 0.0)[:1] for row in rows]
        for v in range((k0 + PANEL) // 8, n):
            a[v] = jnp.where(in_panel, 0.0, a[v])
            c = solve(cols[v])
            for j in range(PANEL):
                a[v] = a[v] - c[j] * rows[j]
    return out


def store_rows(ref, at, rows):
    for i, row in enumerate(rows):
        ref[at + i : at + i + 1, :HALF] = row


def factor_kernel(g_ref, x_ref, t_ref):
    at = 2 * COLS
    g11, g21, g22 = (g_ref[at + i * HALF : at + (i + 1) * HALF, :] for i in range(3))
    store_rows(x_ref, 0, inverse_factor_128(g11))
    x_ref[:HALF, HALF:] = jnp.zeros((HALF, HALF), F32)
    x11 = x_ref[:HALF, :HALF]
    l21 = dot6(g21, x11, NT)
    store_rows(t_ref, 0, inverse_factor_128(g22 - dot6(l21, l21, NT)))
    x22 = t_ref[...]
    x_ref[HALF:, HALF:] = x22
    x_ref[HALF:, :HALF] = -dot6(x22, dot6(l21, x11, NN), NN)


def inverse_factor(reflected):
    return call(
        factor_kernel,
        shape(RANK, RANK),
        reflected,
        flops=2 * 10**10,
        scratch_shapes=[pltpu.VMEM((HALF, HALF), F32)],
    )


def basis_kernel(p_ref, c_ref, x_ref, q_ref, r_ref, s_ref):
    x = split(x_ref[...])
    q_ref[...] = dot3(split(p_ref[...]), x, NT)
    r = dot3(split(get_reflected(c_ref)), x, NT)
    r_ref[...] = r
    squares = jnp.sum(r * r, axis=0, keepdims=True)
    for h in range(2):
        half = squares[:, h * HALF : (h + 1) * HALF]
        s_ref[:, 4 * h : 4 * h + 4, :] = jnp.broadcast_to(half[None], (TP, 4, HALF))


def basis(p, c, x):
    return call(
        basis_kernel,
        (shape(ROWS, RANK), shape(COLS, RANK), shape(TP, 8, HALF)),
        p,
        c,
        x,
        flops=6 * (ROWS + COLS) * RANK * RANK,
    )


def momentum_kernel(g_ref, m_ref, q_ref, r_ref, out_ref):
    product = dot3(split(r_ref[...]), split(q_ref[...]), NT)
    out_ref[...] = (m_ref[...] + g_ref[...]) - (1.0 - decay_rate) * product


def update_kernel(q_ref, r_ref, s_ref, out_ref, d_ref):
    squares = jnp.sum(s_ref[...], axis=0)
    scale = lax.rsqrt(squares / N_COLS + epsilon)
    scale = jnp.concatenate([scale[:1], scale[4:5]], axis=1)
    d = r_ref[...] * scale
    d_ref[...] = d
    out_ref[...] = math.sqrt(M_ROWS / RANK) * dot3(split(d), split(q_ref[...]), NT)


def local(gradient, momentum, start_basis):
    gradient, momentum = gradient.T, momentum.T
    high, low, *p = first(gradient, momentum, start_basis)
    p, _ = tp_sum(*p)
    c = reflect(high, low, p)
    c = fsdp_sum(c)
    p = project(high, low, c)
    p, x = tp_sum(*p, inverse_factor(c))
    p, c = second_reflect(high, low, p, x)
    c = fsdp_sum(c)
    x = inverse_factor(c)
    q, r, squares = basis(p, c, x)
    squares = lax.all_to_all(squares, "tp", 0, 0)
    flops = 6 * ROWS * COLS * RANK
    new_momentum = call(momentum_kernel, shape(COLS, ROWS), gradient, momentum, q, r, flops=flops)
    update, directions = call(
        update_kernel, (shape(COLS, ROWS), shape(COLS, RANK)), q, r, squares, flops=flops
    )
    return (update.T, new_momentum.T, directions)


def solution(mesh):
    return jax.shard_map(
        local,
        mesh=mesh,
        in_specs=(P("fsdp", "tp"), P("fsdp", "tp"), P("tp", None)),
        out_specs=(P("fsdp", "tp"), P("fsdp", "tp"), P("tp", None)),
        check_vma=False,
    )
```

```python
import math

import jax
import jax.numpy as jnp
from jax import lax
from jax.experimental import pallas as pl
from jax.experimental.pallas import tpu as pltpu
from jax.sharding import PartitionSpec as P

M_ROWS = 18432
N_COLS = 7168
RANK = 256
HALF = RANK // 2
FSDP = 32
TP = 16
ROWS = M_ROWS // FSDP
COLS = N_COLS // TP
BAND = 2 * ROWS // TP
PACKED = 2 * COLS + 3 * HALF

decay_rate = 0.95
epsilon = 1e-06

F32 = jnp.float32
BF16 = jnp.bfloat16
HIGHEST = lax.Precision.HIGHEST
PANEL = 8

NN = (((1,), (0,)), ((), ()))
NT = (((1,), (1,)), ((), ()))
TN = (((0,), (0,)), ((), ()))


def split(x):
    high = x.astype(BF16)
    return high, (x - high.astype(F32)).astype(BF16)


def dot3(a, b, dims):
    one = lambda u, v: lax.dot_general(u, v, dims, preferred_element_type=F32)
    return one(a[0], b[0]) + (one(a[0], b[1]) + one(a[1], b[0]))


def dot6(a, b, dims):
    return lax.dot_general(a, b, dims, precision=HIGHEST, preferred_element_type=F32)


def call(kernel, out_shape, *args, flops=0, vmem=48, **kw):
    n_bytes = sum(x.size * x.dtype.itemsize for x in args)
    return pl.pallas_call(
        kernel,
        out_shape=out_shape,
        compiler_params=pltpu.CompilerParams(vmem_limit_bytes=vmem * 2**20),
        cost_estimate=pl.CostEstimate(flops=flops, bytes_accessed=n_bytes, transcendentals=0),
        **kw,
    )(*args)


def shape(*dims, dtype=F32):
    return jax.ShapeDtypeStruct(dims, dtype)


def put_halves(own_ref, other_ref, value):
    left, right = value[:, :HALF], value[:, HALF:]
    even = lax.rem(lax.axis_index("tp"), 2) == 0
    own_ref[...] = jnp.where(even, left, right)
    other_ref[...] = jnp.where(even, right, left)


def get_bands(ref):
    halves = [ref[pl.ds(h, TP // 2, 2)] for h in range(2)]
    return jnp.concatenate([x.reshape(ROWS, HALF) for x in halves], axis=1)


def first_kernel(a_ref, b_ref, high_ref, low_ref, own_ref, other_ref):
    high, low = split(a_ref[...])
    high_ref[...] = high
    low_ref[...] = low
    put_halves(own_ref, other_ref, dot3((high, low), split(b_ref[...]), TN))


def first(a, b):
    wide = shape(COLS, ROWS, dtype=BF16)
    half = shape(ROWS, HALF)
    return call(first_kernel, (wide, wide, half, half), a, b, flops=6 * ROWS * COLS * RANK)


def add_kernel(x_ref, out_ref):
    out_ref[...] = jnp.sum(x_ref[...], axis=0)


def repeat_kernel(x_ref, y_ref, out_ref):
    out_ref[...] = jnp.broadcast_to((x_ref[...] + y_ref[...])[None], out_ref.shape)


def fsdp_sum(x):
    chips = FSDP // 2
    places = [list(range(core, FSDP, 2)) for core in range(2)]
    rows = x.shape[0] // chips
    terms = lax.all_to_all(x.reshape(chips, rows, HALF), "fsdp", 0, 0, axis_index_groups=places)
    piece = call(add_kernel, shape(rows, HALF), terms)
    other = lax.ppermute(piece, "fsdp", [(i, i ^ 1) for i in range(FSDP)])
    pieces = call(repeat_kernel, shape(chips, rows, HALF), piece, other)
    pieces = lax.all_to_all(pieces, "fsdp", 0, 0, axis_index_groups=places)
    return pieces.reshape(chips * rows, HALF)


def tp_sum(own, other, beside=None):
    own = own + lax.ppermute(other, "tp", [(i, i ^ 1) for i in range(TP)])
    places = [list(range(i, TP, 2)) for i in range(2)]
    terms = lax.all_to_all(own.reshape(TP // 2, BAND, HALF), "tp", 0, 0, axis_index_groups=places)
    band = call(add_kernel, shape(BAND, HALF), terms)
    if beside is not None:
        band, beside = lax.optimization_barrier((band, beside))
    return lax.all_gather(band, "tp"), beside


def put_reflected(ref, c, p):
    for h in range(2):
        ref[h * COLS : (h + 1) * COLS, :] = c[:, h * HALF : (h + 1) * HALF]
    left, right = p[:, :HALF], p[:, HALF:]
    for i, (a, b) in enumerate(((left, left), (right, left), (right, right))):
        ref[2 * COLS + i * HALF : 2 * COLS + (i + 1) * HALF, :] = dot6(a, b, TN)


def get_reflected(ref):
    return jnp.concatenate([ref[h * COLS : (h + 1) * COLS, :] for h in range(2)], axis=1)


def reflect_kernel(high_ref, low_ref, p_ref, out_ref):
    p = get_bands(p_ref)
    put_reflected(out_ref, dot3((high_ref[...], low_ref[...]), split(p), NN), p)


def reflect(high, low, p):
    return call(reflect_kernel, shape(PACKED, HALF), high, low, p, flops=6 * ROWS * COLS * RANK)


def project_kernel(high_ref, low_ref, c_ref, own_ref, other_ref):
    c = split(get_reflected(c_ref))
    put_halves(own_ref, other_ref, dot3((high_ref[...], low_ref[...]), c, TN))


def project(high, low, c):
    half = shape(ROWS, HALF)
    return call(project_kernel, (half, half), high, low, c, flops=6 * ROWS * COLS * RANK)


def second_reflect_kernel(high_ref, low_ref, p_ref, x_ref, p_out_ref, out_ref):
    p = dot3(split(get_bands(p_ref)), split(x_ref[...]), NT)
    p_out_ref[...] = p
    put_reflected(out_ref, dot3((high_ref[...], low_ref[...]), split(p), NN), p)


def second_reflect(high, low, p, x):
    return call(
        second_reflect_kernel,
        (shape(ROWS, RANK), shape(PACKED, HALF)),
        high,
        low,
        p,
        x,
        flops=6 * ROWS * COLS * RANK,
    )


def inverse_factor_128(s):
    lanes = lambda v, k: jnp.broadcast_to(v[:, k : k + 1], (8, HALF))
    sublanes = lambda v, k: jnp.broadcast_to(v[k : k + 1, :], (8, HALF))
    n = HALF // 8
    col_at = lax.broadcasted_iota(jnp.int32, (8, HALF), 1)
    a = [s[8 * v : 8 * v + 8, :] for v in range(n)]
    out = []
    for k0 in range(0, HALF, PANEL):
        place = [divmod(k0 + j, 8) for j in range(PANEL)]
        in_panel = (col_at >= k0) & (col_at < k0 + PANEL)
        cols = {v: [lanes(a[v], k0 + j) for j in range(PANEL)] for v in range(k0 // 8, n)}
        rows = [
            jnp.where(in_panel, jnp.where(col_at == k0 + j, 1.0, 0.0), sublanes(a[v], k))
            for j, (v, k) in enumerate(place)
        ]
        d = [[sublanes(cols[v][j], k) for j in range(i + 1)] for i, (v, k) in enumerate(place)]
        factor = [[None] * PANEL for _ in range(PANEL)]
        inverse = [None] * PANEL
        for j in range(PANEL):
            t = d[j][j]
            for k in range(j):
                t = t - factor[j][k] * factor[j][k]
            inverse[j] = lax.rsqrt(t)
            for i in range(j + 1, PANEL):
                t = d[i][j]
                for k in range(j):
                    t = t - factor[i][k] * factor[j][k]
                factor[i][j] = t * inverse[j]

        def solve(x):
            y = []
            for j in range(PANEL):
                t = x[j]
                for k in range(j):
                    t = t - factor[j][k] * y[k]
                y.append(t * inverse[j])
            return y

        rows = solve(rows)
        out += [jnp.where(col_at < k0 + PANEL, row, 0.0)[:1] for row in rows]
        for v in range((k0 + PANEL) // 8, n):
            a[v] = jnp.where(in_panel, 0.0, a[v])
            c = solve(cols[v])
            for j in range(PANEL):
                a[v] = a[v] - c[j] * rows[j]
    return out


def store_rows(ref, at, rows):
    for i, row in enumerate(rows):
        ref[at + i : at + i + 1, :HALF] = row


def factor_kernel(g_ref, x_ref, t_ref):
    at = 2 * COLS
    g11, g21, g22 = (g_ref[at + i * HALF : at + (i + 1) * HALF, :] for i in range(3))
    store_rows(x_ref, 0, inverse_factor_128(g11))
    x_ref[:HALF, HALF:] = jnp.zeros((HALF, HALF), F32)
    x11 = x_ref[:HALF, :HALF]
    l21 = dot6(g21, x11, NT)
    store_rows(t_ref, 0, inverse_factor_128(g22 - dot6(l21, l21, NT)))
    x22 = t_ref[...]
    x_ref[HALF:, HALF:] = x22
    x_ref[HALF:, :HALF] = -dot6(x22, dot6(l21, x11, NN), NN)


def inverse_factor(reflected):
    return call(
        factor_kernel,
        shape(RANK, RANK),
        reflected,
        flops=2 * 10**10,
        scratch_shapes=[pltpu.VMEM((HALF, HALF), F32)],
    )


def basis_kernel(p_ref, c_ref, x_ref, q_ref, r_ref, s_ref):
    x = split(x_ref[...])
    q_ref[...] = dot3(split(p_ref[...]), x, NT)
    r = dot3(split(get_reflected(c_ref)), x, NT)
    r_ref[...] = r
    squares = jnp.sum(r * r, axis=0, keepdims=True)
    for h in range(2):
        half = squares[:, h * HALF : (h + 1) * HALF]
        s_ref[:, 4 * h : 4 * h + 4, :] = jnp.broadcast_to(half[None], (TP, 4, HALF))


def basis(p, c, x):
    return call(
        basis_kernel,
        (shape(ROWS, RANK), shape(COLS, RANK), shape(TP, 8, HALF)),
        p,
        c,
        x,
        flops=6 * (ROWS + COLS) * RANK * RANK,
    )


def momentum_kernel(a_ref, q_ref, r_ref, out_ref):
    product = dot3(split(r_ref[...]), split(q_ref[...]), NT)
    out_ref[...] = a_ref[...] - (1.0 - decay_rate) * product


def update_kernel(q_ref, r_ref, s_ref, out_ref, d_ref):
    squares = jnp.sum(s_ref[...], axis=0)
    scale = lax.rsqrt(squares / N_COLS + epsilon)
    scale = jnp.concatenate([scale[:1], scale[4:5]], axis=1)
    d = r_ref[...] * scale
    d_ref[...] = d
    out_ref[...] = math.sqrt(M_ROWS / RANK) * dot3(split(d), split(q_ref[...]), NT)


def local(gradient, momentum, start_basis):
    combined = momentum.T + gradient.T
    high, low, *p = first(combined, start_basis)
    p, _ = tp_sum(*p)
    c = reflect(high, low, p)
    c = fsdp_sum(c)
    p = project(high, low, c)
    p, x = tp_sum(*p, inverse_factor(c))
    p, c = second_reflect(high, low, p, x)
    c = fsdp_sum(c)
    x = inverse_factor(c)
    q, r, squares = basis(p, c, x)
    squares = lax.all_to_all(squares, "tp", 0, 0)
    flops = 6 * ROWS * COLS * RANK
    new_momentum = call(momentum_kernel, shape(COLS, ROWS), combined, q, r, flops=flops)
    update, directions = call(
        update_kernel, (shape(COLS, ROWS), shape(COLS, RANK)), q, r, squares, flops=flops
    )
    return (update.T, new_momentum.T, directions)


def solution(mesh):
    return jax.shard_map(
        local,
        mesh=mesh,
        in_specs=(P("fsdp", "tp"), P("fsdp", "tp"), P("tp", None)),
        out_specs=(P("fsdp", "tp"), P("fsdp", "tp"), P("tp", None)),
        check_vma=False,
    )
```

```python
import math

import jax
import jax.numpy as jnp
from jax import lax
from jax.experimental import pallas as pl
from jax.experimental.pallas import tpu as pltpu
from jax.sharding import PartitionSpec as P

M_ROWS = 18432
N_COLS = 7168
RANK = 256
HALF = RANK // 2
FSDP = 32
TP = 16
ROWS = M_ROWS // FSDP
COLS = N_COLS // TP
BAND = 2 * ROWS // TP
PACKED = 2 * COLS + 3 * HALF

decay_rate = 0.95
epsilon = 1e-06

F32 = jnp.float32
BF16 = jnp.bfloat16
HIGHEST = lax.Precision.HIGHEST
PANEL = 8

NN = (((1,), (0,)), ((), ()))
NT = (((1,), (1,)), ((), ()))
TN = (((0,), (0,)), ((), ()))


def split(x):
    high = x.astype(BF16)
    return high, (x - high.astype(F32)).astype(BF16)


def dot3(a, b, dims):
    one = lambda u, v: lax.dot_general(u, v, dims, preferred_element_type=F32)
    return one(a[0], b[0]) + (one(a[0], b[1]) + one(a[1], b[0]))


def dot6(a, b, dims):
    return lax.dot_general(a, b, dims, precision=HIGHEST, preferred_element_type=F32)


def call(kernel, out_shape, *args, flops=0, vmem=48, **kw):
    n_bytes = sum(x.size * x.dtype.itemsize for x in args)
    return pl.pallas_call(
        kernel,
        out_shape=out_shape,
        compiler_params=pltpu.CompilerParams(vmem_limit_bytes=vmem * 2**20),
        cost_estimate=pl.CostEstimate(flops=flops, bytes_accessed=n_bytes, transcendentals=0),
        **kw,
    )(*args)


def shape(*dims, dtype=F32):
    return jax.ShapeDtypeStruct(dims, dtype)


def put_halves(own_ref, other_ref, value):
    left, right = value[:, :HALF], value[:, HALF:]
    even = lax.rem(lax.axis_index("tp"), 2) == 0
    own_ref[...] = jnp.where(even, left, right)
    other_ref[...] = jnp.where(even, right, left)


def get_bands(ref):
    halves = [ref[pl.ds(h, TP // 2, 2)] for h in range(2)]
    return jnp.concatenate([x.reshape(ROWS, HALF) for x in halves], axis=1)


def first_kernel(a_ref, b_ref, high_ref, low_ref, own_ref, other_ref):
    high, low = split(a_ref[...])
    high_ref[...] = high
    low_ref[...] = low
    put_halves(own_ref, other_ref, dot3((high, low), split(b_ref[...]), TN))


def first(a, b):
    wide = shape(COLS, ROWS, dtype=BF16)
    half = shape(ROWS, HALF)
    return call(first_kernel, (wide, wide, half, half), a, b, flops=6 * ROWS * COLS * RANK)


def add_kernel(x_ref, out_ref):
    out_ref[...] = jnp.sum(x_ref[...], axis=0)


def repeat_kernel(x_ref, y_ref, out_ref):
    out_ref[...] = jnp.broadcast_to((x_ref[...] + y_ref[...])[None], out_ref.shape)


def fsdp_sum(x):
    chips = FSDP // 2
    places = [list(range(core, FSDP, 2)) for core in range(2)]
    rows = x.shape[0] // chips
    terms = lax.all_to_all(x.reshape(chips, rows, HALF), "fsdp", 0, 0, axis_index_groups=places)
    piece = call(add_kernel, shape(rows, HALF), terms)
    other = lax.ppermute(piece, "fsdp", [(i, i ^ 1) for i in range(FSDP)])
    pieces = call(repeat_kernel, shape(chips, rows, HALF), piece, other)
    pieces = lax.all_to_all(pieces, "fsdp", 0, 0, axis_index_groups=places)
    return pieces.reshape(chips * rows, HALF)


def tp_sum(own, other, beside=None):
    own = own + lax.ppermute(other, "tp", [(i, i ^ 1) for i in range(TP)])
    places = [list(range(i, TP, 2)) for i in range(2)]
    terms = lax.all_to_all(own.reshape(TP // 2, BAND, HALF), "tp", 0, 0, axis_index_groups=places)
    band = call(add_kernel, shape(BAND, HALF), terms)
    if beside is not None:
        band, beside = lax.optimization_barrier((band, beside))
    return lax.all_gather(band, "tp"), beside


def put_reflected(ref, c, p):
    for h in range(2):
        ref[h * COLS : (h + 1) * COLS, :] = c[:, h * HALF : (h + 1) * HALF]
    gram = dot6(p, p, TN)
    for i, (a, b) in enumerate(((0, 0), (HALF, 0), (HALF, HALF))):
        ref[2 * COLS + i * HALF : 2 * COLS + (i + 1) * HALF, :] = gram[a : a + HALF, b : b + HALF]


def get_reflected(ref):
    return jnp.concatenate([ref[h * COLS : (h + 1) * COLS, :] for h in range(2)], axis=1)


def reflect_kernel(high_ref, low_ref, p_ref, out_ref):
    p = get_bands(p_ref)
    put_reflected(out_ref, dot3((high_ref[...], low_ref[...]), split(p), NN), p)


def reflect(high, low, p):
    return call(reflect_kernel, shape(PACKED, HALF), high, low, p, flops=6 * ROWS * COLS * RANK)


def project_kernel(high_ref, low_ref, c_ref, own_ref, other_ref):
    c = split(get_reflected(c_ref))
    put_halves(own_ref, other_ref, dot3((high_ref[...], low_ref[...]), c, TN))


def project(high, low, c):
    half = shape(ROWS, HALF)
    return call(project_kernel, (half, half), high, low, c, flops=6 * ROWS * COLS * RANK)


def second_reflect_kernel(high_ref, low_ref, p_ref, x_ref, p_out_ref, out_ref):
    p = dot3(split(get_bands(p_ref)), split(x_ref[...]), NT)
    p_out_ref[...] = p
    put_reflected(out_ref, dot3((high_ref[...], low_ref[...]), split(p), NN), p)


def second_reflect(high, low, p, x):
    return call(
        second_reflect_kernel,
        (shape(ROWS, RANK), shape(PACKED, HALF)),
        high,
        low,
        p,
        x,
        flops=6 * ROWS * COLS * RANK,
    )


def inverse_factor_128(s):
    lanes = lambda v, k: jnp.broadcast_to(v[:, k : k + 1], (8, HALF))
    sublanes = lambda v, k: jnp.broadcast_to(v[k : k + 1, :], (8, HALF))
    n = HALF // 8
    col_at = lax.broadcasted_iota(jnp.int32, (8, HALF), 1)
    a = [s[8 * v : 8 * v + 8, :] for v in range(n)]
    out = []
    for k0 in range(0, HALF, PANEL):
        place = [divmod(k0 + j, 8) for j in range(PANEL)]
        in_panel = (col_at >= k0) & (col_at < k0 + PANEL)
        cols = {v: [lanes(a[v], k0 + j) for j in range(PANEL)] for v in range(k0 // 8, n)}
        rows = [
            jnp.where(in_panel, jnp.where(col_at == k0 + j, 1.0, 0.0), sublanes(a[v], k))
            for j, (v, k) in enumerate(place)
        ]
        d = [[sublanes(cols[v][j], k) for j in range(i + 1)] for i, (v, k) in enumerate(place)]
        factor = [[None] * PANEL for _ in range(PANEL)]
        inverse = [None] * PANEL
        for j in range(PANEL):
            t = d[j][j]
            for k in range(j):
                t = t - factor[j][k] * factor[j][k]
            inverse[j] = lax.rsqrt(t)
            for i in range(j + 1, PANEL):
                t = d[i][j]
                for k in range(j):
                    t = t - factor[i][k] * factor[j][k]
                factor[i][j] = t * inverse[j]

        def solve(x):
            y = []
            for j in range(PANEL):
                t = x[j]
                for k in range(j):
                    t = t - factor[j][k] * y[k]
                y.append(t * inverse[j])
            return y

        rows = solve(rows)
        out += [jnp.where(col_at < k0 + PANEL, row, 0.0)[:1] for row in rows]
        for v in range((k0 + PANEL) // 8, n):
            a[v] = jnp.where(in_panel, 0.0, a[v])
            c = solve(cols[v])
            for j in range(PANEL):
                a[v] = a[v] - c[j] * rows[j]
    return out


def store_rows(ref, at, rows):
    for i, row in enumerate(rows):
        ref[at + i : at + i + 1, :HALF] = row


def factor_kernel(g_ref, x_ref, t_ref):
    at = 2 * COLS
    g11, g21, g22 = (g_ref[at + i * HALF : at + (i + 1) * HALF, :] for i in range(3))
    store_rows(x_ref, 0, inverse_factor_128(g11))
    x_ref[:HALF, HALF:] = jnp.zeros((HALF, HALF), F32)
    x11 = x_ref[:HALF, :HALF]
    l21 = dot6(g21, x11, NT)
    store_rows(t_ref, 0, inverse_factor_128(g22 - dot6(l21, l21, NT)))
    x22 = t_ref[...]
    x_ref[HALF:, HALF:] = x22
    x_ref[HALF:, :HALF] = -dot6(x22, dot6(l21, x11, NN), NN)


def inverse_factor(reflected):
    return call(
        factor_kernel,
        shape(RANK, RANK),
        reflected,
        flops=2 * 10**10,
        scratch_shapes=[pltpu.VMEM((HALF, HALF), F32)],
    )


def squares_kernel(c_ref, x_ref, s_ref):
    r = dot3(split(get_reflected(c_ref)), split(x_ref[...]), NT)
    squares = jnp.sum(r * r, axis=0, keepdims=True)
    for h in range(2):
        half = squares[:, h * HALF : (h + 1) * HALF]
        s_ref[:, 4 * h : 4 * h + 4, :] = jnp.broadcast_to(half[None], (TP, 4, HALF))


def basis_kernel(p_ref, c_ref, x_ref, high_ref, low_ref, r_ref):
    x = split(x_ref[...])
    high_ref[...], low_ref[...] = split(dot3(split(p_ref[...]), x, NT))
    r_ref[...] = dot3(split(get_reflected(c_ref)), x, NT)


def basis(p, c, x):
    half = shape(ROWS, RANK, dtype=BF16)
    flops = 6 * (ROWS + COLS) * RANK * RANK
    return call(basis_kernel, (half, half, shape(COLS, RANK)), p, c, x, flops=flops)


def momentum_kernel(a_ref, high_ref, low_ref, r_ref, out_ref):
    product = dot3(split(r_ref[...]), (high_ref[...], low_ref[...]), NT)
    out_ref[...] = a_ref[...] - (1.0 - decay_rate) * product


def update_kernel(high_ref, low_ref, r_ref, s_ref, out_ref, d_ref):
    squares = jnp.sum(s_ref[...], axis=0)
    scale = lax.rsqrt(squares / N_COLS + epsilon)
    scale = jnp.concatenate([scale[:1], scale[4:5]], axis=1)
    d = r_ref[...] * scale
    d_ref[...] = d
    product = dot3(split(d), (high_ref[...], low_ref[...]), NT)
    out_ref[...] = math.sqrt(M_ROWS / RANK) * product


def local(gradient, momentum, start_basis):
    combined = momentum.T + gradient.T
    high, low, *p = first(combined, start_basis)
    p, _ = tp_sum(*p)
    c = reflect(high, low, p)
    c = fsdp_sum(c)
    p = project(high, low, c)
    p, x = tp_sum(*p, inverse_factor(c))
    p, c = second_reflect(high, low, p, x)
    c = fsdp_sum(c)
    x = inverse_factor(c)
    squares = call(squares_kernel, shape(TP, 8, HALF), c, x, flops=6 * COLS * RANK * RANK)
    squares = lax.all_to_all(squares, "tp", 0, 0)
    *q, r = basis(p, c, x)
    flops = 6 * ROWS * COLS * RANK
    new_momentum = call(momentum_kernel, shape(COLS, ROWS), combined, *q, r, flops=flops)
    update, directions = call(
        update_kernel, (shape(COLS, ROWS), shape(COLS, RANK)), *q, r, squares, flops=flops
    )
    return (update.T, new_momentum.T, directions)


def solution(mesh):
    return jax.shard_map(
        local,
        mesh=mesh,
        in_specs=(P("fsdp", "tp"), P("fsdp", "tp"), P("tp", None)),
        out_specs=(P("fsdp", "tp"), P("fsdp", "tp"), P("tp", None)),
        check_vma=False,
    )
```

```python
import math

import jax
import jax.numpy as jnp
from jax import lax
from jax.experimental import pallas as pl
from jax.experimental.pallas import tpu as pltpu
from jax.sharding import PartitionSpec as P

M_ROWS = 18432
N_COLS = 7168
RANK = 256
HALF = RANK // 2
FSDP = 32
TP = 16
ROWS = M_ROWS // FSDP
COLS = N_COLS // TP
BAND = 2 * ROWS // TP
PACKED = 2 * COLS + 3 * HALF

decay_rate = 0.95
epsilon = 1e-06

F32 = jnp.float32
BF16 = jnp.bfloat16
HIGHEST = lax.Precision.HIGHEST
PANEL = 8

NN = (((1,), (0,)), ((), ()))
NT = (((1,), (1,)), ((), ()))
TN = (((0,), (0,)), ((), ()))


def split(x):
    high = x.astype(BF16)
    return high, (x - high.astype(F32)).astype(BF16)


def dot3(a, b, dims):
    one = lambda u, v: lax.dot_general(u, v, dims, preferred_element_type=F32)
    return one(a[0], b[0]) + (one(a[0], b[1]) + one(a[1], b[0]))


def dot6(a, b, dims):
    return lax.dot_general(a, b, dims, precision=HIGHEST, preferred_element_type=F32)


def call(kernel, out_shape, *args, flops=0, vmem=48, **kw):
    n_bytes = sum(x.size * x.dtype.itemsize for x in args)
    return pl.pallas_call(
        kernel,
        out_shape=out_shape,
        compiler_params=pltpu.CompilerParams(vmem_limit_bytes=vmem * 2**20),
        cost_estimate=pl.CostEstimate(flops=flops, bytes_accessed=n_bytes, transcendentals=0),
        **kw,
    )(*args)


def shape(*dims, dtype=F32):
    return jax.ShapeDtypeStruct(dims, dtype)


def put_halves(own_ref, other_ref, value):
    left, right = value[:, :HALF], value[:, HALF:]
    even = lax.rem(lax.axis_index("tp"), 2) == 0
    own_ref[...] = jnp.where(even, left, right)
    other_ref[...] = jnp.where(even, right, left)


def get_bands(ref):
    halves = [ref[pl.ds(h, TP // 2, 2)] for h in range(2)]
    return jnp.concatenate([x.reshape(ROWS, HALF) for x in halves], axis=1)


def first_kernel(a_ref, b_ref, high_ref, low_ref, own_ref, other_ref):
    high, low = split(a_ref[...])
    high_ref[...] = high
    low_ref[...] = low
    put_halves(own_ref, other_ref, dot3((high, low), split(b_ref[...]), TN))


def first(a, b):
    wide = shape(COLS, ROWS, dtype=BF16)
    half = shape(ROWS, HALF)
    return call(first_kernel, (wide, wide, half, half), a, b, flops=6 * ROWS * COLS * RANK)


def add_kernel(x_ref, out_ref):
    out_ref[...] = jnp.sum(x_ref[...], axis=0)


def repeat_kernel(x_ref, y_ref, out_ref):
    out_ref[...] = jnp.broadcast_to((x_ref[...] + y_ref[...])[None], out_ref.shape)


def fsdp_sum(x):
    chips = FSDP // 2
    places = [list(range(core, FSDP, 2)) for core in range(2)]
    rows = x.shape[0] // chips
    terms = lax.all_to_all(x.reshape(chips, rows, HALF), "fsdp", 0, 0, axis_index_groups=places)
    piece = call(add_kernel, shape(rows, HALF), terms)
    other = lax.ppermute(piece, "fsdp", [(i, i ^ 1) for i in range(FSDP)])
    pieces = call(repeat_kernel, shape(chips, rows, HALF), piece, other)
    pieces = lax.all_to_all(pieces, "fsdp", 0, 0, axis_index_groups=places)
    return pieces.reshape(chips * rows, HALF)


def tp_sum(own, other, beside=None):
    own = own + lax.ppermute(other, "tp", [(i, i ^ 1) for i in range(TP)])
    places = [list(range(i, TP, 2)) for i in range(2)]
    terms = lax.all_to_all(own.reshape(TP // 2, BAND, HALF), "tp", 0, 0, axis_index_groups=places)
    band = call(add_kernel, shape(BAND, HALF), terms)
    if beside is not None:
        band, beside = lax.optimization_barrier((band, beside))
    return lax.all_gather(band, "tp"), beside


def put_reflected(ref, c, p):
    for h in range(2):
        ref[h * COLS : (h + 1) * COLS, :] = c[:, h * HALF : (h + 1) * HALF]
    gram = dot6(p, p, TN)
    for i, (a, b) in enumerate(((0, 0), (HALF, 0), (HALF, HALF))):
        ref[2 * COLS + i * HALF : 2 * COLS + (i + 1) * HALF, :] = gram[a : a + HALF, b : b + HALF]


def get_reflected(ref):
    return jnp.concatenate([ref[h * COLS : (h + 1) * COLS, :] for h in range(2)], axis=1)


def reflect_kernel(high_ref, low_ref, p_ref, out_ref):
    p = get_bands(p_ref)
    put_reflected(out_ref, dot3((high_ref[...], low_ref[...]), split(p), NN), p)


def reflect(high, low, p):
    return call(reflect_kernel, shape(PACKED, HALF), high, low, p, flops=6 * ROWS * COLS * RANK)


def project_kernel(high_ref, low_ref, c_ref, own_ref, other_ref):
    c = split(get_reflected(c_ref))
    put_halves(own_ref, other_ref, dot3((high_ref[...], low_ref[...]), c, TN))


def project(high, low, c):
    half = shape(ROWS, HALF)
    return call(project_kernel, (half, half), high, low, c, flops=6 * ROWS * COLS * RANK)


def second_reflect_kernel(high_ref, low_ref, p_ref, x_ref, p_out_ref, out_ref):
    p = dot3(split(get_bands(p_ref)), split(x_ref[...]), NT)
    p_out_ref[...] = p
    put_reflected(out_ref, dot3((high_ref[...], low_ref[...]), split(p), NN), p)


def second_reflect(high, low, p, x):
    return call(
        second_reflect_kernel,
        (shape(ROWS, RANK), shape(PACKED, HALF)),
        high,
        low,
        p,
        x,
        flops=6 * ROWS * COLS * RANK,
    )


def inverse_factor_128(s):
    lanes = lambda v, k: jnp.broadcast_to(v[:, k : k + 1], (8, HALF))
    sublanes = lambda v, k: jnp.broadcast_to(v[k : k + 1, :], (8, HALF))
    n = HALF // 8
    col_at = lax.broadcasted_iota(jnp.int32, (8, HALF), 1)
    a = [s[8 * v : 8 * v + 8, :] for v in range(n)]
    out = []
    for k0 in range(0, HALF, PANEL):
        place = [divmod(k0 + j, 8) for j in range(PANEL)]
        in_panel = (col_at >= k0) & (col_at < k0 + PANEL)
        cols = {v: [lanes(a[v], k0 + j) for j in range(PANEL)] for v in range(k0 // 8, n)}
        rows = [
            jnp.where(in_panel, jnp.where(col_at == k0 + j, 1.0, 0.0), sublanes(a[v], k))
            for j, (v, k) in enumerate(place)
        ]
        d = [[sublanes(cols[v][j], k) for j in range(i + 1)] for i, (v, k) in enumerate(place)]
        factor = [[None] * PANEL for _ in range(PANEL)]
        inverse = [None] * PANEL
        for j in range(PANEL):
            t = d[j][j]
            for k in range(j):
                t = t - factor[j][k] * factor[j][k]
            inverse[j] = lax.rsqrt(t)
            for i in range(j + 1, PANEL):
                t = d[i][j]
                for k in range(j):
                    t = t - factor[i][k] * factor[j][k]
                factor[i][j] = t * inverse[j]

        def solve(x):
            y = []
            for j in range(PANEL):
                t = x[j]
                for k in range(j):
                    t = t - factor[j][k] * y[k]
                y.append(t * inverse[j])
            return y

        rows = solve(rows)
        out += [jnp.where(col_at < k0 + PANEL, row, 0.0)[:1] for row in rows]
        for v in range((k0 + PANEL) // 8, n):
            a[v] = jnp.where(in_panel, 0.0, a[v])
            c = solve(cols[v])
            for j in range(PANEL):
                a[v] = a[v] - c[j] * rows[j]
    return out


def store_rows(ref, at, rows):
    for i, row in enumerate(rows):
        ref[at + i : at + i + 1, :HALF] = row


def factor_kernel(g_ref, x_ref, t_ref):
    at = 2 * COLS
    g11, g21, g22 = (g_ref[at + i * HALF : at + (i + 1) * HALF, :] for i in range(3))
    store_rows(x_ref, 0, inverse_factor_128(g11))
    x_ref[:HALF, HALF:] = jnp.zeros((HALF, HALF), F32)
    x11 = x_ref[:HALF, :HALF]
    l21 = dot6(g21, x11, NT)
    store_rows(t_ref, 0, inverse_factor_128(g22 - dot6(l21, l21, NT)))
    x22 = t_ref[...]
    x_ref[HALF:, HALF:] = x22
    x_ref[HALF:, :HALF] = -dot6(x22, dot6(l21, x11, NN), NN)


def inverse_factor(reflected):
    return call(
        factor_kernel,
        shape(RANK, RANK),
        reflected,
        flops=2 * 10**10,
        scratch_shapes=[pltpu.VMEM((HALF, HALF), F32)],
    )


def basis_kernel(p_ref, c_ref, x_ref, q_ref, r_ref, s_ref):
    x = split(x_ref[...])
    q_ref[...] = dot3(split(p_ref[...]), x, NT)
    r = dot3(split(get_reflected(c_ref)), x, NT)
    r_ref[...] = r
    squares = jnp.sum(r * r, axis=0, keepdims=True)
    for h in range(2):
        half = squares[:, h * HALF : (h + 1) * HALF]
        s_ref[:, 4 * h : 4 * h + 4, :] = jnp.broadcast_to(half[None], (TP, 4, HALF))


def basis(p, c, x):
    return call(
        basis_kernel,
        (shape(ROWS, RANK), shape(COLS, RANK), shape(TP, 8, HALF)),
        p,
        c,
        x,
        flops=6 * (ROWS + COLS) * RANK * RANK,
    )


def momentum_kernel(a_ref, q_ref, r_ref, out_ref):
    product = dot3(split(r_ref[...]), split(q_ref[...]), NT)
    out_ref[...] = a_ref[...] - (1.0 - decay_rate) * product


def update_kernel(q_ref, r_ref, s_ref, out_ref, d_ref):
    squares = jnp.sum(s_ref[...], axis=0)
    scale = lax.rsqrt(squares / N_COLS + epsilon)
    scale = jnp.concatenate([scale[:1], scale[4:5]], axis=1)
    d = r_ref[...] * scale
    d_ref[...] = d
    out_ref[...] = math.sqrt(M_ROWS / RANK) * dot3(split(d), split(q_ref[...]), NT)


def local(gradient, momentum, start_basis):
    combined = momentum.T + gradient.T
    high, low, *p = first(combined, start_basis)
    p, _ = tp_sum(*p)
    c = reflect(high, low, p)
    c = fsdp_sum(c)
    p = project(high, low, c)
    p, x = tp_sum(*p, inverse_factor(c))
    p, c = second_reflect(high, low, p, x)
    c = fsdp_sum(c)
    x = inverse_factor(c)
    q, r, squares = basis(p, c, x)
    squares = lax.all_to_all(squares, "tp", 0, 0)
    flops = 6 * ROWS * COLS * RANK
    new_momentum = call(momentum_kernel, shape(COLS, ROWS), combined, q, r, flops=flops)
    update, directions = call(
        update_kernel, (shape(COLS, ROWS), shape(COLS, RANK)), q, r, squares, flops=flops
    )
    return (update.T, new_momentum.T, directions)


def solution(mesh):
    return jax.shard_map(
        local,
        mesh=mesh,
        in_specs=(P("fsdp", "tp"), P("fsdp", "tp"), P("tp", None)),
        out_specs=(P("fsdp", "tp"), P("fsdp", "tp"), P("tp", None)),
        check_vma=False,
    )
```

```python
import functools
import math

import jax
import jax.numpy as jnp
from jax import lax
from jax.experimental import pallas as pl
from jax.experimental.pallas import tpu as pltpu
from jax.sharding import PartitionSpec as P

M_ROWS = 18432
N_COLS = 7168
RANK = 256
HALF = RANK // 2
FSDP = 32
TP = 16
ROWS = M_ROWS // FSDP
COLS = N_COLS // TP
BAND = 2 * ROWS // TP
PACKED = 2 * COLS + 3 * HALF

decay_rate = 0.95
epsilon = 1e-06

F32 = jnp.float32
BF16 = jnp.bfloat16
HIGHEST = lax.Precision.HIGHEST
PANEL = 8

NN = (((1,), (0,)), ((), ()))
NT = (((1,), (1,)), ((), ()))
TN = (((0,), (0,)), ((), ()))


def split(x):
    high = x.astype(BF16)
    return high, (x - high.astype(F32)).astype(BF16)


def dot3(a, b, dims):
    one = lambda u, v: lax.dot_general(u, v, dims, preferred_element_type=F32)
    return one(a[0], b[0]) + (one(a[0], b[1]) + one(a[1], b[0]))


def dot6(a, b, dims):
    return lax.dot_general(a, b, dims, precision=HIGHEST, preferred_element_type=F32)


def call(kernel, out_shape, *args, flops=0, vmem=48, **kw):
    n_bytes = sum(x.size * x.dtype.itemsize for x in args)
    return pl.pallas_call(
        kernel,
        out_shape=out_shape,
        compiler_params=pltpu.CompilerParams(vmem_limit_bytes=vmem * 2**20),
        cost_estimate=pl.CostEstimate(flops=flops, bytes_accessed=n_bytes, transcendentals=0),
        **kw,
    )(*args)


def shape(*dims, dtype=F32):
    return jax.ShapeDtypeStruct(dims, dtype)


def half_of(x, own):
    even = lax.rem(lax.axis_index("tp"), 2) == 0
    left, right = x[:, :HALF], x[:, HALF:]
    return jnp.where(even, left, right) if own else jnp.where(even, right, left)


def get_bands(ref):
    halves = [ref[pl.ds(h, TP // 2, 2)] for h in range(2)]
    return jnp.concatenate([x.reshape(ROWS, HALF) for x in halves], axis=1)


def first_kernel(a_ref, b_ref, high_ref, low_ref, other_ref):
    high, low = split(a_ref[...])
    high_ref[...] = high
    low_ref[...] = low
    other_ref[...] = dot3((high, low), split(half_of(b_ref[...], False)), TN)


def first(a, b):
    wide = shape(COLS, ROWS, dtype=BF16)
    half = shape(ROWS, HALF)
    return call(first_kernel, (wide, wide, half), a, b, flops=3 * ROWS * COLS * RANK)


def first_own_kernel(high_ref, low_ref, b_ref, own_ref):
    own_ref[...] = dot3((high_ref[...], low_ref[...]), split(half_of(b_ref[...], True)), TN)


def add_kernel(x_ref, out_ref):
    out_ref[...] = jnp.sum(x_ref[...], axis=0)


def repeat_kernel(x_ref, y_ref, out_ref):
    out_ref[...] = jnp.broadcast_to((x_ref[...] + y_ref[...])[None], out_ref.shape)


def fsdp_sum(x):
    chips = FSDP // 2
    places = [list(range(core, FSDP, 2)) for core in range(2)]
    rows = x.shape[0] // chips
    terms = lax.all_to_all(x.reshape(chips, rows, HALF), "fsdp", 0, 0, axis_index_groups=places)
    piece = call(add_kernel, shape(rows, HALF), terms)
    other = lax.ppermute(piece, "fsdp", [(i, i ^ 1) for i in range(FSDP)])
    pieces = call(repeat_kernel, shape(chips, rows, HALF), piece, other)
    pieces = lax.all_to_all(pieces, "fsdp", 0, 0, axis_index_groups=places)
    return pieces.reshape(chips * rows, HALF)


def tp_sum(own, other, beside=None):
    own = own + lax.ppermute(other, "tp", [(i, i ^ 1) for i in range(TP)])
    places = [list(range(i, TP, 2)) for i in range(2)]
    terms = lax.all_to_all(own.reshape(TP // 2, BAND, HALF), "tp", 0, 0, axis_index_groups=places)
    band = call(add_kernel, shape(BAND, HALF), terms)
    if beside is not None:
        band, beside = lax.optimization_barrier((band, beside))
    return lax.all_gather(band, "tp"), beside


def put_reflected(ref, c, p):
    for h in range(2):
        ref[h * COLS : (h + 1) * COLS, :] = c[:, h * HALF : (h + 1) * HALF]
    gram = dot6(p, p, TN)
    for i, (a, b) in enumerate(((0, 0), (HALF, 0), (HALF, HALF))):
        ref[2 * COLS + i * HALF : 2 * COLS + (i + 1) * HALF, :] = gram[a : a + HALF, b : b + HALF]


def get_reflected(ref):
    return jnp.concatenate([ref[h * COLS : (h + 1) * COLS, :] for h in range(2)], axis=1)


def reflect_kernel(high_ref, low_ref, p_ref, out_ref):
    p = get_bands(p_ref)
    put_reflected(out_ref, dot3((high_ref[...], low_ref[...]), split(p), NN), p)


def reflect(high, low, p):
    return call(reflect_kernel, shape(PACKED, HALF), high, low, p, flops=6 * ROWS * COLS * RANK)


def project_kernel(own, high_ref, low_ref, c_ref, out_ref):
    c = split(half_of(get_reflected(c_ref), own))
    out_ref[...] = dot3((high_ref[...], low_ref[...]), c, TN)


def project(high, low, c, own):
    kernel = functools.partial(project_kernel, own)
    return call(kernel, shape(ROWS, HALF), high, low, c, flops=3 * ROWS * COLS * RANK)


def second_reflect_kernel(high_ref, low_ref, p_ref, x_ref, p_out_ref, out_ref):
    p = dot3(split(get_bands(p_ref)), split(x_ref[...]), NT)
    p_out_ref[...] = p
    put_reflected(out_ref, dot3((high_ref[...], low_ref[...]), split(p), NN), p)


def second_reflect(high, low, p, x):
    return call(
        second_reflect_kernel,
        (shape(ROWS, RANK), shape(PACKED, HALF)),
        high,
        low,
        p,
        x,
        flops=6 * ROWS * COLS * RANK,
    )


def inverse_factor_128(s):
    lanes = lambda v, k: jnp.broadcast_to(v[:, k : k + 1], (8, HALF))
    sublanes = lambda v, k: jnp.broadcast_to(v[k : k + 1, :], (8, HALF))
    n = HALF // 8
    col_at = lax.broadcasted_iota(jnp.int32, (8, HALF), 1)
    a = [s[8 * v : 8 * v + 8, :] for v in range(n)]
    out = []
    for k0 in range(0, HALF, PANEL):
        place = [divmod(k0 + j, 8) for j in range(PANEL)]
        in_panel = (col_at >= k0) & (col_at < k0 + PANEL)
        cols = {v: [lanes(a[v], k0 + j) for j in range(PANEL)] for v in range(k0 // 8, n)}
        rows = [
            jnp.where(in_panel, jnp.where(col_at == k0 + j, 1.0, 0.0), sublanes(a[v], k))
            for j, (v, k) in enumerate(place)
        ]
        d = [[sublanes(cols[v][j], k) for j in range(i + 1)] for i, (v, k) in enumerate(place)]
        factor = [[None] * PANEL for _ in range(PANEL)]
        inverse = [None] * PANEL
        for j in range(PANEL):
            t = d[j][j]
            for k in range(j):
                t = t - factor[j][k] * factor[j][k]
            inverse[j] = lax.rsqrt(t)
            for i in range(j + 1, PANEL):
                t = d[i][j]
                for k in range(j):
                    t = t - factor[i][k] * factor[j][k]
                factor[i][j] = t * inverse[j]

        def solve(x):
            y = []
            for j in range(PANEL):
                t = x[j]
                for k in range(j):
                    t = t - factor[j][k] * y[k]
                y.append(t * inverse[j])
            return y

        rows = solve(rows)
        out += [jnp.where(col_at < k0 + PANEL, row, 0.0)[:1] for row in rows]
        for v in range((k0 + PANEL) // 8, n):
            a[v] = jnp.where(in_panel, 0.0, a[v])
            c = solve(cols[v])
            for j in range(PANEL):
                a[v] = a[v] - c[j] * rows[j]
    return out


def store_rows(ref, at, rows):
    for i, row in enumerate(rows):
        ref[at + i : at + i + 1, :HALF] = row


def factor_kernel(g_ref, x_ref, t_ref):
    at = 2 * COLS
    g11, g21, g22 = (g_ref[at + i * HALF : at + (i + 1) * HALF, :] for i in range(3))
    store_rows(x_ref, 0, inverse_factor_128(g11))
    x_ref[:HALF, HALF:] = jnp.zeros((HALF, HALF), F32)
    x11 = x_ref[:HALF, :HALF]
    l21 = dot6(g21, x11, NT)
    store_rows(t_ref, 0, inverse_factor_128(g22 - dot6(l21, l21, NT)))
    x22 = t_ref[...]
    x_ref[HALF:, HALF:] = x22
    x_ref[HALF:, :HALF] = -dot6(x22, dot6(l21, x11, NN), NN)


def inverse_factor(reflected):
    return call(
        factor_kernel,
        shape(RANK, RANK),
        reflected,
        flops=2 * 10**10,
        scratch_shapes=[pltpu.VMEM((HALF, HALF), F32)],
    )


def basis_kernel(p_ref, c_ref, x_ref, q_ref, r_ref, s_ref):
    x = split(x_ref[...])
    q_ref[...] = dot3(split(p_ref[...]), x, NT)
    r = dot3(split(get_reflected(c_ref)), x, NT)
    r_ref[...] = r
    squares = jnp.sum(r * r, axis=0, keepdims=True)
    for h in range(2):
        half = squares[:, h * HALF : (h + 1) * HALF]
        s_ref[:, 4 * h : 4 * h + 4, :] = jnp.broadcast_to(half[None], (TP, 4, HALF))


def basis(p, c, x):
    return call(
        basis_kernel,
        (shape(ROWS, RANK), shape(COLS, RANK), shape(TP, 8, HALF)),
        p,
        c,
        x,
        flops=6 * (ROWS + COLS) * RANK * RANK,
    )


def momentum_kernel(a_ref, q_ref, r_ref, out_ref):
    product = dot3(split(r_ref[...]), split(q_ref[...]), NT)
    out_ref[...] = a_ref[...] - (1.0 - decay_rate) * product


def update_kernel(q_ref, r_ref, s_ref, out_ref, d_ref):
    squares = jnp.sum(s_ref[...], axis=0)
    scale = lax.rsqrt(squares / N_COLS + epsilon)
    scale = jnp.concatenate([scale[:1], scale[4:5]], axis=1)
    d = r_ref[...] * scale
    d_ref[...] = d
    out_ref[...] = math.sqrt(M_ROWS / RANK) * dot3(split(d), split(q_ref[...]), NT)


def local(gradient, momentum, start_basis):
    combined = momentum.T + gradient.T
    high, low, other = first(combined, start_basis)
    flops = 3 * ROWS * COLS * RANK
    own = call(first_own_kernel, shape(ROWS, HALF), high, low, start_basis, flops=flops)
    p, _ = tp_sum(own, other)
    c = reflect(high, low, p)
    c = fsdp_sum(c)
    other, own = project(high, low, c, False), project(high, low, c, True)
    p, x = tp_sum(own, other, inverse_factor(c))
    p, c = second_reflect(high, low, p, x)
    c = fsdp_sum(c)
    x = inverse_factor(c)
    q, r, squares = basis(p, c, x)
    squares = lax.all_to_all(squares, "tp", 0, 0)
    flops = 6 * ROWS * COLS * RANK
    new_momentum = call(momentum_kernel, shape(COLS, ROWS), combined, q, r, flops=flops)
    update, directions = call(
        update_kernel, (shape(COLS, ROWS), shape(COLS, RANK)), q, r, squares, flops=flops
    )
    return (update.T, new_momentum.T, directions)


def solution(mesh):
    return jax.shard_map(
        local,
        mesh=mesh,
        in_specs=(P("fsdp", "tp"), P("fsdp", "tp"), P("tp", None)),
        out_specs=(P("fsdp", "tp"), P("fsdp", "tp"), P("tp", None)),
        check_vma=False,
    )
```
